32 devices in a mesh: grp: 2 (over x), ex: 16 (over z, y, core).
Axes of the slice: x: 2, y: 2, z: 4, core: 2. Of those that a mesh axis runs over, the one named last changes fastest.
Arguments:
- query_factors: bfloat16 [1, 2, 4096, 128], P(None, None, None, 'ex'), may hold values from -6 to 6
- eigen_basis: bfloat16 [1, 2, 4096, 4096], P(None, None, None, 'ex'), may hold values from -0.09375 to 0.09375
- eigen_values: float32 [1, 2, 4096], P(None, None, 'ex'), may hold values from 0.05 to 20
- train_factors: bfloat16 [1, 2, 4096, 16384], P(None, None, None, ('grp', 'ex')), parts along dimension 3, may hold values from -0.046875 to 0.046875
Outputs:
- scores: float32 [16, 512], P(None, ('grp', 'ex')), parts along dimension 1
The draws below stay inside these ranges and needn't reach their ends.
There are 2 independent parts, one for each index of `grp`. The reference program is written for one: setup_inputs(seed, part) draws one part's arguments, and reference() takes and returns one part's arrays. A program takes and returns all parts, laid end to end along the dimension named above; an argument that names none is the same for every part. Nothing has to cross between parts.
All inputs are finite; a program needn't handle non-finite values.
Results may differ from the reference program's by a relative error of at most 0.004.
Values may be sent and summed in bfloat16 or wider, within the bound.
A program may use at most 64 MiB of HBM per device.

```python
import math
import jax
import jax.numpy as jnp
from jax import lax

D = 4096
LAYERS = 1
RANK = 32
QRANK = 8
QUERIES = 16
QRANKS = 128
TRAIN = 256
TCOLS = 8192


def levels(key, extent, cuts, low, largest):
    factor_of = 1.0
    for axis_at, blocks in cuts:
        heights = jax.random.uniform(jax.random.fold_in(jax.random.fold_in(key, 6), axis_at), (blocks,), jnp.float32, low / len(cuts), largest / len(cuts))
        factor_of = factor_of * jnp.repeat(jnp.exp(heights), extent[axis_at] // blocks).reshape((-1,) + (1,) * (len(extent) - 1 - axis_at))
    return factor_of


def normal_values(key, shape, width, limit, cuts=(), kind=jnp.bfloat16):
    gain = levels(key, shape, cuts, -0.22, 0.18) if cuts else 1.0
    result = jax.random.normal(key, shape, jnp.float32) * width * gain
    return jnp.minimum(jnp.maximum(result, -limit), limit).astype(kind)


def setup_inputs(seed: int = 0, part: int = 0) -> dict:
    key_of = jax.random.split(jax.random.key(seed), 5)
    part_splits = jax.random.split(jax.random.fold_in(key_of[4], part), 5)
    return {
        "query_factors": normal_values(key_of[0], (LAYERS, 2, D, QRANKS), 1.0, 6.0, ((3, 16),)),
        "eigen_basis": normal_values(key_of[1], (LAYERS, 2, D, D), D ** -0.5, 0.09375, ((3, 16),)),
        "eigen_values": jnp.clip(jnp.exp(math.log(20.0) - 5.9914645 * jax.random.uniform(key_of[2], (LAYERS, 2, D), jnp.float32) ** levels(key_of[2], (LAYERS, 2, D), ((2, 16),), -0.2, 0.2)), 0.05, 20.0),
        "train_factors": normal_values(part_splits[3], (LAYERS, 2, D, TCOLS), (4 * D) ** -0.5, 0.046875, ((3, 16),)),
    }


damping_term = 0.1

def reference(query_factors, eigen_basis, eigen_values, train_factors):
    total = jnp.zeros((QUERIES, TRAIN), jnp.float32)
    for layer in range(LAYERS):
        grams = []
        for side in range(2):
            product = jnp.dot(eigen_basis[layer, side].T, query_factors[layer, side], preferred_element_type=jnp.float32)
            scale = 1.0 / (eigen_values[layer, side] + damping_term)
            rotated = (product * scale[:, None]).astype(jnp.bfloat16)
            grams.append(jnp.dot(rotated.T, train_factors[layer, side], preferred_element_type=jnp.float32))
        joined = (grams[0] * grams[1]).reshape(QUERIES, QRANK, TRAIN, RANK)
        total = total + lax.optimization_barrier(jnp.sum(joined, axis=(1, 3)))
    return total * (1.0 / math.sqrt(LAYERS * QRANK * RANK))
```

```python
import functools
import math

import jax
import jax.numpy as jnp
from jax import lax
from jax.experimental import pallas as pl
from jax.experimental.pallas import tpu as pltpu
from jax.sharding import PartitionSpec as P

LAYERS = 1
RANK = 32
QRANK = 8
DAMPING = 0.1
MESH = pl.DeviceIdType.MESH


def flipped(a, bits, count):
    step = 1
    while step < count:
        if bits & step:
            a = a + step - 2 * step * ((a // step) % 2)
        step *= 2
    return a


def kernel(
    nz, q_hbm, basis_hbm, values_ref, train_hbm, out_ref,
    q_in, q_all, basis, train, rot_all, gram, local_sem,
    q_recv, q_send_z, q_send_y, q_send_c,
    r_recv, r_send_z, r_send_y, r_send_x, r_send_c,
):
    grp = lax.axis_index("grp")
    mine = lax.axis_index("ex")
    core = mine % 2
    y = (mine // 2) % 2
    z = mine // 4
    side = grp % 2
    other = 1 - side
    partner = grp + 1 - 2 * side
    n = 4 * nz

    def at(zz, yy, cc):
        return (zz * 2 + yy) * 2 + cc

    zs = [flipped(z, j, nz) for j in range(nz)]
    z_dev = [(grp, at(zs[j], y, core)) for j in range(nz)]
    y_dev = (grp, at(z, 1 - y, core))
    c_dev = (grp, at(z, y, 1 - core))
    x_dev = (partner, mine)

    q_copy = pltpu.make_async_copy(q_hbm.at[side], q_in, local_sem.at[0])
    q_copy.start()
    basis_copy = pltpu.make_async_copy(basis_hbm.at[0, side], basis, local_sem.at[1])
    basis_copy.start()
    train_copy = pltpu.make_async_copy(train_hbm.at[0], train, local_sem.at[2])
    train_copy.start()

    barrier = pltpu.get_barrier_semaphore()
    partners = z_dev[1:] + [y_dev, c_dev, x_dev]
    for device in partners:
        pl.semaphore_signal(barrier, inc=1, device_id=device, device_id_type=MESH)

    q_copy.wait()
    half = q_in.shape[1] // 2
    whole = q_in[...].astype(jnp.float32)
    stacked = jnp.concatenate([whole[:, :half], whole[:, half:]], axis=0)
    q_all[mine] = stacked.astype(q_all.dtype)

    pl.semaphore_wait(barrier, len(partners))

    started = []

    def send(slot, send_sem, recv_sem, device):
        copy = pltpu.make_async_remote_copy(
            src_ref=slot, dst_ref=slot, send_sem=send_sem, recv_sem=recv_sem,
            device_id=device, device_id_type=MESH,
        )
        copy.start()
        started.append(copy)

    def arrived(slot, recv_sem, device):
        pltpu.make_async_remote_copy(
            src_ref=slot, dst_ref=slot, send_sem=local_sem.at[0], recv_sem=recv_sem,
            device_id=device, device_id_type=MESH,
        ).wait_recv()

    def q_send(e, send_sem, device):
        send(q_all.at[e], send_sem, q_recv.at[e], device)

    def q_arrived(e, device):
        arrived(q_all.at[e], q_recv.at[e], device)

    for j in range(1, nz):
        q_send(mine, q_send_z.at[j], z_dev[j])
    for j in range(nz):
        e = at(zs[j], y, core)
        if j:
            q_arrived(e, z_dev[j])
        q_send(e, q_send_y.at[j], y_dev)
        q_send(e, q_send_c.at[j], c_dev)
    for j in range(nz):
        e = at(zs[j], 1 - y, core)
        q_arrived(e, y_dev)
        q_send(e, q_send_c.at[nz + j], c_dev)
    for yy in range(2):
        for j in range(nz):
            q_arrived(at(zs[j], flipped(y, yy, 2), 1 - core), c_dev)

    basis_copy.wait()
    width = basis.shape[1]
    rows = q_all[...].reshape(n * 16, half)
    low = jnp.dot(rows, basis[:half], preferred_element_type=jnp.float32)
    high = jnp.dot(rows, basis[half:], preferred_element_type=jnp.float32)
    product = low.reshape(n, 2, 8, width)[:, 0] + high.reshape(n, 2, 8, width)[:, 1]
    scale = 1.0 / (values_ref[pl.ds(side, 1), :] + DAMPING)
    rotated = product.reshape(n * 8, width) * scale
    rot_all[side, mine] = rotated.astype(rot_all.dtype)

    def r_send(s, e, send_sem, device):
        send(rot_all.at[s, e], send_sem, r_recv.at[s, e], device)

    def r_arrived(s, e, device):
        arrived(rot_all.at[s, e], r_recv.at[s, e], device)

    def add(s, e):
        rows = train[s, pl.ds(pl.multiple_of(e * width, width), width), :]
        gram[s] += jnp.dot(rot_all[s, e], rows, preferred_element_type=jnp.float32)

    cut = nz // 2
    for j in range(1, nz):
        r_send(side, mine, r_send_z.at[j], z_dev[j])
    gram[...] = jnp.zeros_like(gram)
    train_copy.wait()
    for j in range(nz):
        e = at(zs[j], y, core)
        if j:
            r_arrived(side, e, z_dev[j])
        r_send(side, e, r_send_x.at[j], x_dev)
        r_send(side, e, r_send_y.at[j], y_dev)
        r_send(side, e, r_send_c.at[j], c_dev)
        add(side, e)
    for j in range(nz):
        e = at(zs[j], y, core)
        r_arrived(other, e, x_dev)
        if j >= cut:
            r_send(other, e, r_send_y.at[nz + j], y_dev)
        r_send(other, e, r_send_c.at[nz + j], c_dev)
        add(other, e)
        e = at(zs[j], 1 - y, core)
        r_arrived(side, e, y_dev)
        if j < cut:
            r_send(side, e, r_send_x.at[nz + j], x_dev)
        r_send(side, e, r_send_c.at[2 * nz + j], c_dev)
        add(side, e)
    for j in range(nz):
        e = at(zs[j], 1 - y, core)
        r_arrived(other, e, x_dev if j < cut else y_dev)
        r_send(other, e, r_send_c.at[3 * nz + j], c_dev)
        add(other, e)
    for s, yy in ((side, y), (other, y), (side, 1 - y), (other, 1 - y)):
        for j in range(nz):
            e = at(zs[j], yy, 1 - core)
            r_arrived(s, e, c_dev)
            add(s, e)

    joined = gram[0] * gram[1]
    columns = joined.shape[1]
    by_query = jnp.sum(joined.reshape(joined.shape[0] // QRANK, QRANK, columns), axis=1)
    count_t = columns // RANK
    member = lax.broadcasted_iota(jnp.int32, (columns, count_t), 0) // RANK
    picks = member == lax.broadcasted_iota(jnp.int32, (columns, count_t), 1)
    scores = jnp.dot(
        by_query, picks.astype(jnp.float32), precision=lax.Precision.HIGHEST,
        preferred_element_type=jnp.float32,
    )
    out_ref[...] = scores * (1.0 / math.sqrt(LAYERS * QRANK * RANK))

    for copy in started:
        copy.wait_send()


def per_device(query_factors, eigen_basis, eigen_values, train_factors):
    n = lax.axis_size("ex")
    nz = n // 4
    depth, per = query_factors.shape[2:]
    width = eigen_basis.shape[3]
    tcols = train_factors.shape[3]
    queries = jnp.transpose(query_factors[0], (0, 2, 1))
    hbm = pl.BlockSpec(memory_space=pl.ANY)
    vmem = pl.BlockSpec(memory_space=pltpu.VMEM)
    dma = pltpu.SemaphoreType.DMA
    return pl.pallas_call(
        functools.partial(kernel, nz),
        out_shape=jax.ShapeDtypeStruct((n * per // QRANK, tcols // RANK), jnp.float32),
        in_specs=[hbm, hbm, vmem, hbm],
        out_specs=vmem,
        scratch_shapes=[
            pltpu.VMEM((per, depth), jnp.bfloat16),
            pltpu.VMEM((n, 2 * per, depth // 2), jnp.bfloat16),
            pltpu.VMEM((depth, width), jnp.bfloat16),
            pltpu.VMEM((2, depth, tcols), jnp.bfloat16),
            pltpu.VMEM((2, n, n * per, width), jnp.bfloat16),
            pltpu.VMEM((2, n * per, tcols), jnp.float32),
            dma((3,)),
            dma((n,)), dma((nz,)), dma((nz,)), dma((2 * nz,)),
            dma((2, n)), dma((nz,)), dma((2 * nz,)), dma((2 * nz,)), dma((4 * nz,)),
        ],
        compiler_params=pltpu.CompilerParams(
            collective_id=0, has_side_effects=True, vmem_limit_bytes=56 * 2**20
        ),
    )(queries, eigen_basis, eigen_values[0], train_factors)


def solution(mesh):
    in_specs = (
        P(None, None, None, "ex"),
        P(None, None, None, "ex"),
        P(None, None, "ex"),
        P(None, None, None, ("grp", "ex")),
    )
    out_specs = P(None, ("grp", "ex"))
    return jax.shard_map(
        per_device, mesh=mesh, in_specs=in_specs, out_specs=out_specs, check_vma=False
    )
```

```python
import functools
import math

import jax
import jax.numpy as jnp
from jax import lax
from jax.experimental import pallas as pl
from jax.experimental.pallas import tpu as pltpu
from jax.sharding import PartitionSpec as P

LAYERS = 1
RANK = 32
QRANK = 8
DAMPING = 0.1
MESH = pl.DeviceIdType.MESH


def flipped(a, bits, count):
    step = 1
    while step < count:
        if bits & step:
            a = a + step - 2 * step * ((a // step) % 2)
        step *= 2
    return a


def kernel(
    nz, q_hbm, basis_hbm, values_hbm, train_hbm, out_ref,
    values_ref, q_in, q_all, basis, train, rot_all, gram, local_sem,
    q_recv, q_send_z, q_send_y, q_send_c,
    r_recv, r_send_z, r_send_y, r_send_x, r_send_c,
):
    grp = lax.axis_index("grp")
    mine = lax.axis_index("ex")
    core = mine % 2
    y = (mine // 2) % 2
    z = mine // 4
    side = grp % 2
    other = 1 - side
    partner = grp + 1 - 2 * side
    n = 4 * nz

    def at(zz, yy, cc):
        return (zz * 2 + yy) * 2 + cc

    zs = [flipped(z, j, nz) for j in range(nz)]
    z_dev = [(grp, at(zs[j], y, core)) for j in range(nz)]
    y_dev = (grp, at(z, 1 - y, core))
    c_dev = (grp, at(z, y, 1 - core))
    x_dev = (partner, mine)

    barrier = pltpu.get_barrier_semaphore()
    partners = z_dev[1:] + [y_dev, c_dev, x_dev]
    for device in partners:
        pl.semaphore_signal(barrier, inc=1, device_id=device, device_id_type=MESH)

    q_copy = pltpu.make_async_copy(q_hbm.at[side], q_in, local_sem.at[0])
    q_copy.start()
    basis_copy = pltpu.make_async_copy(basis_hbm.at[0, side], basis, local_sem.at[1])
    basis_copy.start()
    values_copy = pltpu.make_async_copy(values_hbm, values_ref, local_sem.at[3])
    values_copy.start()
    train_copy = pltpu.make_async_copy(train_hbm.at[0], train, local_sem.at[2])
    train_copy.start()

    q_copy.wait()
    half = q_in.shape[1] // 2
    whole = q_in[...].astype(jnp.float32)
    stacked = jnp.concatenate([whole[:, :half], whole[:, half:]], axis=0)
    q_all[mine] = stacked.astype(q_all.dtype)

    pl.semaphore_wait(barrier, len(partners))

    started = []

    def send(slot, send_sem, recv_sem, device):
        copy = pltpu.make_async_remote_copy(
            src_ref=slot, dst_ref=slot, send_sem=send_sem, recv_sem=recv_sem,
            device_id=device, device_id_type=MESH,
        )
        copy.start()
        started.append(copy)

    def arrived(slot, recv_sem, device):
        pltpu.make_async_remote_copy(
            src_ref=slot, dst_ref=slot, send_sem=local_sem.at[0], recv_sem=recv_sem,
            device_id=device, device_id_type=MESH,
        ).wait_recv()

    def q_send(e, send_sem, device):
        send(q_all.at[e], send_sem, q_recv.at[e], device)

    def q_arrived(e, device):
        arrived(q_all.at[e], q_recv.at[e], device)

    for j in range(1, nz):
        q_send(mine, q_send_z.at[j], z_dev[j])
    for j in range(nz):
        e = at(zs[j], y, core)
        if j:
            q_arrived(e, z_dev[j])
        q_send(e, q_send_y.at[j], y_dev)
        q_send(e, q_send_c.at[j], c_dev)
    for j in range(nz):
        e = at(zs[j], 1 - y, core)
        q_arrived(e, y_dev)
        q_send(e, q_send_c.at[nz + j], c_dev)
    for yy in range(2):
        for j in range(nz):
            q_arrived(at(zs[j], flipped(y, yy, 2), 1 - core), c_dev)

    basis_copy.wait()
    values_copy.wait()
    width = basis.shape[1]
    rows = q_all[...].reshape(n * 16, half)
    low = jnp.dot(rows, basis[:half], preferred_element_type=jnp.float32)
    high = jnp.dot(rows, basis[half:], preferred_element_type=jnp.float32)
    product = low.reshape(n, 2, 8, width)[:, 0] + high.reshape(n, 2, 8, width)[:, 1]
    scale = 1.0 / (values_ref[pl.ds(side, 1), :] + DAMPING)
    rotated = product.reshape(n * 8, width) * scale
    rot_all[side, mine] = rotated.astype(rot_all.dtype)

    def r_send(s, e, send_sem, device):
        send(rot_all.at[s, e], send_sem, r_recv.at[s, e], device)

    def r_arrived(s, e, device):
        arrived(rot_all.at[s, e], r_recv.at[s, e], device)

    def add(s, e):
        rows = train[s, pl.ds(pl.multiple_of(e * width, width), width), :]
        gram[s] += jnp.dot(rot_all[s, e], rows, preferred_element_type=jnp.float32)

    for j in range(1, nz):
        r_send(side, mine, r_send_z.at[j], z_dev[j])
    for j in range(nz):
        e = at(zs[j], y, core)
        if j:
            r_arrived(side, e, z_dev[j])
        r_send(side, e, r_send_x.at[j], x_dev)
        r_send(side, e, r_send_y.at[j], y_dev)
        r_send(side, e, r_send_c.at[j], c_dev)
        if j == 0:
            gram[...] = jnp.zeros_like(gram)
            train_copy.wait()
        add(side, e)
    for j in range(nz):
        e = at(zs[j], y, core)
        f = at(zs[j], 1 - y, core)
        r_arrived(other, e, x_dev)
        if j % 2:
            r_send(other, e, r_send_y.at[nz + j], y_dev)
        r_send(other, e, r_send_c.at[nz + j], c_dev)
        r_arrived(side, f, y_dev)
        if j % 2 == 0:
            r_send(side, f, r_send_x.at[nz + j], x_dev)
        r_send(side, f, r_send_c.at[2 * nz + j], c_dev)
        add(other, e)
        add(side, f)
    for j in range(nz):
        e = at(zs[j], 1 - y, core)
        r_arrived(other, e, y_dev if j % 2 else x_dev)
        r_send(other, e, r_send_c.at[3 * nz + j], c_dev)
        add(other, e)
    for s, yy in ((side, y), (other, y), (side, 1 - y), (other, 1 - y)):
        for j in range(nz):
            e = at(zs[j], yy, 1 - core)
            r_arrived(s, e, c_dev)
            add(s, e)

    joined = gram[0] * gram[1]
    columns = joined.shape[1]
    by_query = jnp.sum(joined.reshape(joined.shape[0] // QRANK, QRANK, columns), axis=1)
    count_t = columns // RANK
    member = lax.broadcasted_iota(jnp.int32, (columns, count_t), 0) // RANK
    picks = member == lax.broadcasted_iota(jnp.int32, (columns, count_t), 1)
    scores = jnp.dot(
        by_query, picks.astype(jnp.float32), precision=lax.Precision.HIGHEST,
        preferred_element_type=jnp.float32,
    )
    out_ref[...] = scores * (1.0 / math.sqrt(LAYERS * QRANK * RANK))

    for copy in started:
        copy.wait_send()


def per_device(query_factors, eigen_basis, eigen_values, train_factors):
    n = lax.axis_size("ex")
    nz = n // 4
    depth, per = query_factors.shape[2:]
    width = eigen_basis.shape[3]
    tcols = train_factors.shape[3]
    queries = jnp.transpose(query_factors[0], (0, 2, 1))
    hbm = pl.BlockSpec(memory_space=pl.ANY)
    vmem = pl.BlockSpec(memory_space=pltpu.VMEM)
    dma = pltpu.SemaphoreType.DMA
    return pl.pallas_call(
        functools.partial(kernel, nz),
        out_shape=jax.ShapeDtypeStruct((n * per // QRANK, tcols // RANK), jnp.float32),
        in_specs=[hbm, hbm, hbm, hbm],
        out_specs=vmem,
        scratch_shapes=[
            pltpu.VMEM((2, width), jnp.float32),
            pltpu.VMEM((per, depth), jnp.bfloat16),
            pltpu.VMEM((n, 2 * per, depth // 2), jnp.bfloat16),
            pltpu.VMEM((depth, width), jnp.bfloat16),
            pltpu.VMEM((2, depth, tcols), jnp.bfloat16),
            pltpu.VMEM((2, n, n * per, width), jnp.bfloat16),
            pltpu.VMEM((2, n * per, tcols), jnp.float32),
            dma((4,)),
            dma((n,)), dma((nz,)), dma((nz,)), dma((2 * nz,)),
            dma((2, n)), dma((nz,)), dma((2 * nz,)), dma((2 * nz,)), dma((4 * nz,)),
        ],
        compiler_params=pltpu.CompilerParams(
            collective_id=0, has_side_effects=True, vmem_limit_bytes=56 * 2**20
        ),
    )(queries, eigen_basis, eigen_values[0], train_factors)


def solution(mesh):
    in_specs = (
        P(None, None, None, "ex"),
        P(None, None, None, "ex"),
        P(None, None, "ex"),
        P(None, None, None, ("grp", "ex")),
    )
    out_specs = P(None, ("grp", "ex"))
    return jax.shard_map(
        per_device, mesh=mesh, in_specs=in_specs, out_specs=out_specs, check_vma=False
    )
```
